32 devices in a mesh: tm: 8 (over z, x), wall: 4 (over y, core).
Axes of the slice: x: 2, y: 2, z: 4, core: 2. Of those that a mesh axis runs over, the one named last changes fastest.
Arguments:
- start_state: float32 [8, 3, 384, 512], P('tm', None, 'wall'), may hold values from -6 to 6
- end_state: float32 [8, 3, 384, 512], P('tm', None, None, 'wall'), may hold values from -6 to 6
- coupling: float32 [8, 3, 384, 512], P('tm', None, None, 'wall'), may hold values from 0.5 to 1.5
- inverse_ops: float32 [8, 384, 384], P('wall')
- mirror_rows: int32 [384], replicated, may hold values from 0 to 383, as said below
- slab_steps: int32 [8], P('tm'), may hold values from 1 to 8, as said below
Outputs:
- gradient: float32 [8, 3, 384, 512], P('tm', None, 'wall')
The draws below stay inside these ranges and needn't reach their ends.
Inputs may be any that keep to these rules, and one draw needn't show every extreme that they name: mirror_rows is an involution that maps each row of block b = y // 96 to a row of block 3 - b. `slab_steps`: some slab takes 8 steps.
All inputs are finite; a program needn't handle non-finite values.
Results may differ from the reference program's by a relative error of at most 0.00028.
Values sent between devices are 32-bit elements; how exact they have to be, the bound alone decides.
No kernel may reach another device: no remote copies, remote signals or barrier semaphores. Data moves between devices by JAX's collectives and lax.ppermute only.
A program may use at most 64 MiB of HBM per device.

```python
import math
import jax
import jax.numpy as jnp
from jax import lax

NY = 384
STEPS_MAX = 8
ROWS_DEV = 96
GROUPS = 8
MODES = 512
SLABS = 8


def draw_inverse_ops(key, part):
    first, second = jax.random.split(key)
    diagonal = jax.random.uniform(first, (GROUPS, NY), jnp.float32, 0.6, 1.0)
    spread = jax.random.normal(second, (GROUPS, NY, NY), jnp.float32)
    offdiag = spread * (0.35 / math.sqrt(NY))
    return offdiag + diagonal[:, :, None] * jnp.eye(NY, dtype=jnp.float32)[None, :, :]


def draw_mirror_rows(key, part):
    blocks_all = NY // ROWS_DEV
    half = blocks_all // 2
    keys = jax.random.split(key, half)
    perms = jax.vmap(lambda single: jax.random.permutation(single, ROWS_DEV))(keys).astype(jnp.int32)
    inverse = jnp.argsort(perms, axis=1).astype(jnp.int32)
    lower_blocks = jnp.arange(half, dtype=jnp.int32)[:, None]
    lower = (blocks_all - 1 - lower_blocks) * ROWS_DEV + perms
    upper = lower_blocks * ROWS_DEV + inverse
    return jnp.concatenate([lower.reshape(-1), upper[::-1].reshape(-1)]).astype(jnp.int32)


def draw_slab_steps(key, part):
    first, second = jax.random.split(key)
    short_most = max(STEPS_MAX // 4, 1)
    counts = jax.random.randint(first, (SLABS,), 1, short_most + 1)
    chosen = jax.random.randint(second, (), 0, SLABS)
    return jnp.where(jnp.arange(SLABS) == chosen, STEPS_MAX, counts).astype(jnp.int32)


def block_scale(key, shape, cuts, least, largest):
    gain, own = 1.0, jax.random.fold_in(key, 6)
    for axis_at, shards_of in cuts:
        draws = jnp.exp(jax.random.uniform(jax.random.fold_in(own, axis_at), (shards_of,), jnp.float32, least / len(cuts), largest / len(cuts)))
        gain = gain * jnp.repeat(draws, shape[axis_at] // shards_of).reshape([-1 if axis == axis_at else 1 for axis in range(len(shape))])
    return gain


def scatter_about(key, extent, width, bound, cuts=(), held_as=jnp.bfloat16):
    loudness = block_scale(key, extent, cuts, -0.22, 0.18) if cuts else 1.0
    result = jax.random.normal(key, extent, jnp.float32) * width * loudness
    return jnp.minimum(jnp.maximum(result, -bound), bound).astype(held_as)


def setup_inputs(seed: int = 0) -> dict:
    streams_of = jax.random.split(jax.random.key(seed), 7)
    start_state = scatter_about(streams_of[0], (SLABS, 3, NY, MODES), 1.0, 6.0, ((0, 8), (2, 4)), jnp.float32)
    end_state = scatter_about(streams_of[1], (SLABS, 3, NY, MODES), 1.0, 6.0, ((0, 8), (3, 4)), jnp.float32)
    coupling = jnp.clip(jnp.exp(math.log(1.5) - 1.0986123 * jax.random.uniform(streams_of[2], (SLABS, 3, NY, MODES), jnp.float32) ** block_scale(streams_of[2], (SLABS, 3, NY, MODES), ((0, 8), (3, 4)), -0.2, 0.2)), 0.5, 1.5)
    inverse_ops = draw_inverse_ops(jax.random.fold_in(streams_of[6], 71), 0)
    mirror_rows = draw_mirror_rows(jax.random.fold_in(streams_of[6], 71), 0)
    slab_steps = draw_slab_steps(jax.random.fold_in(streams_of[6], 71), 0)
    return {"start_state": start_state, "end_state": end_state, "coupling": coupling, "inverse_ops": inverse_ops, "mirror_rows": mirror_rows, "slab_steps": slab_steps}


def mirror(values, mirror_rows):
    parity = jnp.array([1.0, -1.0, 1.0], jnp.float32).reshape(1, 3, 1, 1)
    return jnp.take(values, mirror_rows, axis=2) * parity


def helmholtz(values, inverse_ops):
    slab_count, components, row_count, col_count = values.shape
    groups = inverse_ops.shape[0]
    blocked = values.reshape(slab_count, components, row_count, groups, col_count // groups)
    product = jnp.einsum("gyz,sczgm->scygm", inverse_ops, blocked, precision=lax.Precision.HIGHEST)
    return product.reshape(values.shape)


def reference(start_state, end_state, coupling, inverse_ops, mirror_rows, slab_steps):
    following = jnp.roll(start_state, -1, axis=0)
    mismatch = end_state - mirror(following, mirror_rows)
    adjoint_state = mismatch
    for position in range(STEPS_MAX):
        advanced = helmholtz(coupling * adjoint_state, inverse_ops)
        active = (position < slab_steps).reshape(-1, 1, 1, 1)
        adjoint_state = jnp.where(active, advanced, adjoint_state)
    earlier = mirror(jnp.roll(mismatch, 1, axis=0), mirror_rows)
    return adjoint_state - earlier
```

```python
import functools

import jax
import jax.numpy as jnp
from jax import lax
from jax.experimental import pallas as pl
from jax.experimental.pallas import tpu as pltpu
from jax.sharding import PartitionSpec as P

STEPS_MAX = 8
LANES = 128
HALF = LANES // 2


def split(values):
    high = values.astype(jnp.bfloat16)
    low = (values - high.astype(jnp.float32)).astype(jnp.bfloat16)
    return high, low


def swap_halves(values):
    return pltpu.roll(values, HALF, 1)


def left_half(shape):
    return lax.broadcasted_iota(jnp.int32, shape, 1) < HALF


def to_groups(first, second):
    left = left_half(first.shape)
    return jnp.where(left, first, swap_halves(second)), jnp.where(left, swap_halves(first), second)


def mirror_block(pieces, mirror_ref, block, rows, count):
    partner = count - 1 - block
    target = mirror_ref[block] - partner * rows
    lane = lax.broadcasted_iota(jnp.int32, (rows, rows), 0)
    one_hot = (lane == target).astype(jnp.bfloat16)
    values = jnp.concatenate(pieces, axis=1)
    high, low = split(values)
    return jnp.dot(
        jnp.concatenate([one_hot, one_hot], axis=1),
        jnp.concatenate([high, low], axis=0),
        preferred_element_type=jnp.float32,
    )


def prepare_kernel(count, rows, wall_ref, mirror_ref, end_ref, ops_ref, *outs):
    wall = wall_ref[0]
    ops_out, sends = outs[0], outs[1:]
    ny = ops_ref.shape[1]
    for group in range(2):
        high, low = split(ops_ref[group])
        ops_out[group, :, 0:ny] = high
        ops_out[group, :, ny : 2 * ny] = high
        ops_out[group, :, 2 * ny : 3 * ny] = low
    for step in range(count):
        source = count - 1 - (wall ^ step)
        at = pl.ds(pl.multiple_of(source * rows, 8), rows)
        moved = mirror_block([end_ref[c, at, :] for c in range(3)], mirror_ref, source, rows, count)
        for c, sign in enumerate((1.0, -1.0, 1.0)):
            sends[step][c] = sign * moved[:, c * LANES : (c + 1) * LANES]


def adjoint_kernel(count, rows, wall_ref, steps_ref, mirror_ref, end_ref, coupling_ref, ops_ref, *rest):
    pieces, outs = rest[:count], rest[count : 2 * count]
    gains, scaled, state = rest[2 * count :]
    wall = wall_ref[0]
    ny = end_ref.shape[1]
    gains[0], gains[1] = to_groups(coupling_ref[0], coupling_ref[1])
    gains[2] = coupling_ref[2]
    for step in range(count):
        block = wall ^ step
        partner = count - 1 - block
        at = pl.ds(pl.multiple_of(partner * rows, 8), rows)
        moved = mirror_block([pieces[step][c] for c in range(3)], mirror_ref, block, rows, count)
        first = end_ref[0, at, :] - moved[:, :LANES]
        second = end_ref[1, at, :] + moved[:, LANES : 2 * LANES]
        state[0, at, :], state[1, at, :] = to_groups(first, second)
        state[2, at, :] = end_ref[2, at, :] - moved[:, 2 * LANES :]

    def advance(_, carry):
        for slot in range(3):
            high, low = split(gains[slot] * state[slot])
            scaled[slot, 0:ny] = high
            scaled[slot, ny : 2 * ny] = low
            scaled[slot, 2 * ny : 3 * ny] = high
        shared = []
        for group in range(2):
            product = jnp.dot(
                ops_ref[group],
                jnp.concatenate([scaled[group], scaled[2]], axis=1),
                preferred_element_type=jnp.float32,
            )
            state[group] = product[:, :LANES]
            shared.append(product[:, LANES:])
        state[2] = jnp.where(left_half(shared[0].shape), shared[0], shared[1])
        return carry

    lax.fori_loop(0, jnp.minimum(steps_ref[0], STEPS_MAX), advance, 0)
    for step in range(count):
        at = pl.ds(pl.multiple_of((wall ^ step) * rows, 8), rows)
        outs[step][0], outs[step][1] = to_groups(state[0, at, :], state[1, at, :])
        outs[step][2] = state[2, at, :]


def combine_kernel(count, wall_ref, start_ref, *rest):
    adjoint_parts, mirrored_parts, out_ref = rest[:count], rest[count : 2 * count], rest[2 * count]
    wall = wall_ref[0]
    for step in range(count):
        at = pl.ds(pl.multiple_of((wall ^ step) * LANES, LANES), LANES)
        out_ref[0, :, at] = adjoint_parts[step][0] - (mirrored_parts[step][0] - start_ref[0, :, at])


def send(parts, steps, shape, first_step=0):
    slabs, count = shape
    moved = []
    for step, part in enumerate(parts):
        step += first_step
        pairs = [
            (t * count + w, (t + steps) % slabs * count + (w ^ step)) for t in range(slabs) for w in range(count)
        ]
        moved.append(lax.ppermute(part, ("tm", "wall"), pairs))
    return moved


def on_device(shape, start_state, end_state, coupling, inverse_ops, mirror_rows, slab_steps):
    slabs, count = shape
    rows = start_state.shape[2]
    ny = end_state.shape[2]
    start, end, gain = start_state[0], end_state[0], coupling[0]
    wall = lax.axis_index("wall").astype(jnp.int32).reshape(1)
    mirror_blocks = mirror_rows.reshape(count, 1, rows)
    smem = pl.BlockSpec(memory_space=pltpu.SMEM)
    vmem = pl.BlockSpec(memory_space=pltpu.VMEM)
    part = jax.ShapeDtypeStruct((3, rows, LANES), jnp.float32)

    outgoing = [
        lax.dynamic_slice(start, (0, 0, (wall[0] ^ step) * LANES), (3, rows, LANES)) for step in range(count)
    ]
    incoming = send(outgoing, -1, shape)

    ops, *mirrored = pl.pallas_call(
        functools.partial(prepare_kernel, count, rows),
        out_shape=[jax.ShapeDtypeStruct((2, ny, 3 * ny), jnp.bfloat16)] + [part] * count,
        in_specs=[smem, vmem, vmem, vmem],
        out_specs=[vmem] * (1 + count),
        compiler_params=pltpu.CompilerParams(vmem_limit_bytes=24 << 20),
        cost_estimate=pl.CostEstimate(flops=10**8, bytes_accessed=4 << 20, transcendentals=0),
        name="prepare",
    )(wall, mirror_blocks, end, inverse_ops)

    mirrored, incoming = lax.optimization_barrier((mirrored, incoming))
    mirrored = send(mirrored, 1, shape)

    adjoint = pl.pallas_call(
        functools.partial(adjoint_kernel, count, rows),
        out_shape=[part] * count,
        in_specs=[smem, smem] + [vmem] * (4 + count),
        out_specs=[vmem] * count,
        scratch_shapes=[
            pltpu.VMEM((3, ny, LANES), jnp.float32),
            pltpu.VMEM((3, 3 * ny, LANES), jnp.bfloat16),
            pltpu.VMEM((3, ny, LANES), jnp.float32),
        ],
        compiler_params=pltpu.CompilerParams(vmem_limit_bytes=24 << 20),
        cost_estimate=pl.CostEstimate(flops=4 * 10**9, bytes_accessed=4 << 20, transcendentals=0),
        name="adjoint",
    )(wall, slab_steps, mirror_blocks, end, gain, ops, *incoming)

    returned = [adjoint[0]]
    for step in range(1, count):
        pairs = [(w, w ^ step) for w in range(count)]
        returned.append(lax.ppermute(adjoint[step], "wall", pairs))

    block = pl.BlockSpec((1, rows, LANES), lambda c: (c, 0, 0))
    whole = pl.BlockSpec((1, rows, count * LANES), lambda c: (c, 0, 0))
    gradient = pl.pallas_call(
        functools.partial(combine_kernel, count),
        grid=(3,),
        out_shape=jax.ShapeDtypeStruct(start.shape, jnp.float32),
        in_specs=[smem, whole] + [block] * (2 * count),
        out_specs=whole,
        compiler_params=pltpu.CompilerParams(vmem_limit_bytes=24 << 20),
        cost_estimate=pl.CostEstimate(flops=10**6, bytes_accessed=3 << 20, transcendentals=0),
        name="combine",
    )(wall, start, *returned, *mirrored)
    return gradient[None]


def solution(mesh):
    in_specs = (
        P("tm", None, "wall", None),
        P("tm", None, None, "wall"),
        P("tm", None, None, "wall"),
        P("wall", None, None),
        P(),
        P("tm"),
    )
    out_specs = P("tm", None, "wall", None)
    shape = (mesh.shape["tm"], mesh.shape["wall"])
    return jax.shard_map(
        functools.partial(on_device, shape),
        mesh=mesh,
        in_specs=in_specs,
        out_specs=out_specs,
        check_vma=False,
    )
```

```python
import functools

import jax
import jax.numpy as jnp
from jax import lax
from jax.experimental import pallas as pl
from jax.experimental.pallas import tpu as pltpu
from jax.sharding import PartitionSpec as P

STEPS_MAX = 8
LANES = 128
HALF = LANES // 2


def split(values):
    high = values.astype(jnp.bfloat16)
    low = (values - high.astype(jnp.float32)).astype(jnp.bfloat16)
    return high, low


def swap_halves(values):
    return pltpu.roll(values, HALF, 1)


def left_half(shape):
    return lax.broadcasted_iota(jnp.int32, shape, 1) < HALF


def to_groups(first, second):
    left = left_half(first.shape)
    return jnp.where(left, first, swap_halves(second)), jnp.where(left, swap_halves(first), second)


def mirror_block(pieces, mirror_ref, block, rows, count):
    partner = count - 1 - block
    target = mirror_ref[block] - partner * rows
    lane = lax.broadcasted_iota(jnp.int32, (rows, rows), 0)
    one_hot = (lane == target).astype(jnp.bfloat16)
    values = jnp.concatenate(pieces, axis=1)
    high, low = split(values)
    return jnp.dot(
        jnp.concatenate([one_hot, one_hot], axis=1),
        jnp.concatenate([high, low], axis=0),
        preferred_element_type=jnp.float32,
    )


def prepare_kernel(count, rows, wall_ref, mirror_ref, end_ref, ops_ref, *outs):
    wall = wall_ref[0]
    ops_out, sends = outs[0], outs[1:]
    ny = ops_ref.shape[1]
    for group in range(2):
        high, low = split(ops_ref[group])
        ops_out[group, :, 0:ny] = high
        ops_out[group, :, ny : 2 * ny] = high
        ops_out[group, :, 2 * ny : 3 * ny] = low
    for step in range(count):
        source = count - 1 - (wall ^ step)
        at = pl.ds(pl.multiple_of(source * rows, 8), rows)
        moved = mirror_block([end_ref[c, at, :] for c in range(3)], mirror_ref, source, rows, count)
        for c, sign in enumerate((1.0, -1.0, 1.0)):
            sends[step][c] = sign * moved[:, c * LANES : (c + 1) * LANES]


def adjoint_kernel(count, rows, wall_ref, steps_ref, mirror_ref, end_ref, coupling_ref, ops_ref, *rest):
    pieces, outs = rest[:count], rest[count : 2 * count]
    gains, scaled, state = rest[2 * count :]
    wall = wall_ref[0]
    ny = end_ref.shape[1]
    gains[0], gains[1] = to_groups(coupling_ref[0], coupling_ref[1])
    gains[2] = coupling_ref[2]
    for step in range(count):
        block = wall ^ step
        partner = count - 1 - block
        at = pl.ds(pl.multiple_of(partner * rows, 8), rows)
        moved = mirror_block([pieces[step][c] for c in range(3)], mirror_ref, block, rows, count)
        first = end_ref[0, at, :] - moved[:, :LANES]
        second = end_ref[1, at, :] + moved[:, LANES : 2 * LANES]
        state[0, at, :], state[1, at, :] = to_groups(first, second)
        state[2, at, :] = end_ref[2, at, :] - moved[:, 2 * LANES :]

    def advance(_, carry):
        for slot in range(3):
            high, low = split(gains[slot] * state[slot])
            scaled[slot, 0:ny] = high
            scaled[slot, ny : 2 * ny] = low
            scaled[slot, 2 * ny : 3 * ny] = high
        shared = []
        for group in range(2):
            product = jnp.dot(
                ops_ref[group],
                jnp.concatenate([scaled[group], scaled[2]], axis=1),
                preferred_element_type=jnp.float32,
            )
            state[group] = product[:, :LANES]
            shared.append(product[:, LANES:])
        state[2] = jnp.where(left_half(shared[0].shape), shared[0], shared[1])
        return carry

    lax.fori_loop(0, jnp.minimum(steps_ref[0], STEPS_MAX), advance, 0)
    for step in range(count):
        at = pl.ds(pl.multiple_of((wall ^ step) * rows, 8), rows)
        outs[step][0], outs[step][1] = to_groups(state[0, at, :], state[1, at, :])
        outs[step][2] = state[2, at, :]


def offset_kernel(count, wall_ref, start_ref, *rest):
    parts, out_ref = rest[:-1], rest[-1]
    wall = wall_ref[0]
    for step, part in enumerate(parts):
        at = pl.ds(pl.multiple_of((wall ^ step) * LANES, LANES), LANES)
        out_ref[:, :, at] = part[...] - start_ref[:, :, at]


def combine_kernel(count, wall_ref, offset_ref, *rest):
    parts, out_ref = rest[:-1], rest[-1]
    wall = wall_ref[0]
    for step, part in enumerate(parts):
        at = pl.ds(pl.multiple_of((wall ^ step) * LANES, LANES), LANES)
        out_ref[:, :, at] = part[...] - offset_ref[:, :, at]


def send(part, steps, flip, shape):
    slabs, count = shape
    pairs = [(t * count + w, (t + steps) % slabs * count + (w ^ flip)) for t in range(slabs) for w in range(count)]
    return lax.ppermute(part, ("tm", "wall"), pairs)


def on_device(shape, start_state, end_state, coupling, inverse_ops, mirror_rows, slab_steps):
    slabs, count = shape
    rows = start_state.shape[2]
    ny = end_state.shape[2]
    start, end, gain = start_state[0], end_state[0], coupling[0]
    wall = lax.axis_index("wall").astype(jnp.int32).reshape(1)
    mirror_blocks = mirror_rows.reshape(count, 1, rows)
    smem = pl.BlockSpec(memory_space=pltpu.SMEM)
    vmem = pl.BlockSpec(memory_space=pltpu.VMEM)
    part = jax.ShapeDtypeStruct((3, rows, LANES), jnp.float32)

    outgoing = [
        lax.dynamic_slice(start, (0, 0, (wall[0] ^ step) * LANES), (3, rows, LANES)) for step in range(count)
    ]
    incoming = [send(part, -1, step, shape) for step, part in enumerate(outgoing)]

    ops, *mirrored = pl.pallas_call(
        functools.partial(prepare_kernel, count, rows),
        out_shape=[jax.ShapeDtypeStruct((2, ny, 3 * ny), jnp.bfloat16)] + [part] * count,
        in_specs=[smem, vmem, vmem, vmem],
        out_specs=[vmem] * (1 + count),
        compiler_params=pltpu.CompilerParams(vmem_limit_bytes=24 << 20),
        cost_estimate=pl.CostEstimate(flops=10**8, bytes_accessed=4 << 20, transcendentals=0),
        name="prepare",
    )(wall, mirror_blocks, end, inverse_ops)

    mirrored, arrived = lax.optimization_barrier((mirrored, incoming[:-1]))
    incoming = arrived + incoming[-1:]
    mirrored = [send(part, 1, i, shape) for i, part in enumerate(mirrored)]

    adjoint = pl.pallas_call(
        functools.partial(adjoint_kernel, count, rows),
        out_shape=[part] * count,
        in_specs=[smem, smem] + [vmem] * (4 + count),
        out_specs=[vmem] * count,
        scratch_shapes=[
            pltpu.VMEM((3, ny, LANES), jnp.float32),
            pltpu.VMEM((3, 3 * ny, LANES), jnp.bfloat16),
            pltpu.VMEM((3, ny, LANES), jnp.float32),
        ],
        compiler_params=pltpu.CompilerParams(vmem_limit_bytes=24 << 20),
        cost_estimate=pl.CostEstimate(flops=4 * 10**9, bytes_accessed=4 << 20, transcendentals=0),
        name="adjoint",
    )(wall, slab_steps, mirror_blocks, end, gain, ops, *incoming)

    returned = [adjoint[0]]
    for step in range(1, count):
        returned.append(send(adjoint[step], 0, step, shape))

    block = pl.BlockSpec((1, rows, LANES), lambda c: (c, 0, 0))
    whole = pl.BlockSpec((1, rows, count * LANES), lambda c: (c, 0, 0))
    offset = pl.pallas_call(
        functools.partial(offset_kernel, count),
        out_shape=jax.ShapeDtypeStruct(start.shape, jnp.float32),
        in_specs=[smem, vmem] + [vmem] * count,
        out_specs=vmem,
        compiler_params=pltpu.CompilerParams(vmem_limit_bytes=24 << 20),
        cost_estimate=pl.CostEstimate(flops=10**6, bytes_accessed=40 << 20, transcendentals=0),
        name="offset",
    )(wall, start, *mirrored)
    gradient = pl.pallas_call(
        functools.partial(combine_kernel, count),
        grid=(3,),
        out_shape=jax.ShapeDtypeStruct(start.shape, jnp.float32),
        in_specs=[smem, whole] + [block] * count,
        out_specs=whole,
        compiler_params=pltpu.CompilerParams(vmem_limit_bytes=24 << 20),
        cost_estimate=pl.CostEstimate(flops=10**6, bytes_accessed=3 << 20, transcendentals=0),
        name="combine",
    )(wall, offset, *returned)
    return gradient[None]


def solution(mesh):
    in_specs = (
        P("tm", None, "wall", None),
        P("tm", None, None, "wall"),
        P("tm", None, None, "wall"),
        P("wall", None, None),
        P(),
        P("tm"),
    )
    out_specs = P("tm", None, "wall", None)
    shape = (mesh.shape["tm"], mesh.shape["wall"])
    return jax.shard_map(
        functools.partial(on_device, shape),
        mesh=mesh,
        in_specs=in_specs,
        out_specs=out_specs,
        check_vma=False,
    )
```

```python
import functools

import jax
import jax.numpy as jnp
from jax import lax
from jax.experimental import pallas as pl
from jax.experimental.pallas import tpu as pltpu
from jax.sharding import PartitionSpec as P

STEPS_MAX = 8
LANES = 128
HALF = LANES // 2


def split(values):
    high = values.astype(jnp.bfloat16)
    low = (values - high.astype(jnp.float32)).astype(jnp.bfloat16)
    return high, low


def swap_halves(values):
    return pltpu.roll(values, HALF, 1)


def left_half(shape):
    return lax.broadcasted_iota(jnp.int32, shape, 1) < HALF


def to_groups(first, second):
    left = left_half(first.shape)
    return jnp.where(left, first, swap_halves(second)), jnp.where(left, swap_halves(first), second)


def mirror_block(pieces, mirror_ref, block, rows, count):
    partner = count - 1 - block
    target = mirror_ref[block] - partner * rows
    lane = lax.broadcasted_iota(jnp.int32, (rows, rows), 0)
    one_hot = (lane == target).astype(jnp.bfloat16)
    values = jnp.concatenate(pieces, axis=1)
    high, low = split(values)
    return jnp.dot(
        jnp.concatenate([one_hot, one_hot], axis=1),
        jnp.concatenate([high, low], axis=0),
        preferred_element_type=jnp.float32,
    )


def prepare_kernel(count, rows, wall_ref, mirror_ref, end_ref, coupling_ref, ops_ref, ops_out, gains, base, *sends):
    wall = wall_ref[0]
    ny = ops_ref.shape[1]
    left = left_half((ny, LANES))
    for group in range(2):
        high, low = split(ops_ref[group])
        ops_out[group, :, 0:ny] = high
        ops_out[group, :, ny : 2 * ny] = high
        ops_out[group, :, 2 * ny : 3 * ny] = low
    gains[0, :, :LANES], gains[1, :, :LANES] = to_groups(coupling_ref[0], coupling_ref[1])
    gains[0, :, LANES:] = jnp.where(left, coupling_ref[2], 0.0)
    gains[1, :, LANES:] = jnp.where(left, 0.0, coupling_ref[2])
    base[0, :, :LANES], base[1, :, :LANES] = to_groups(end_ref[0], end_ref[1])
    base[0, :, LANES:] = end_ref[2]
    base[1, :, LANES:] = end_ref[2]
    for step in range(count):
        source = count - 1 - (wall ^ step)
        at = pl.ds(pl.multiple_of(source * rows, 8), rows)
        moved = mirror_block([end_ref[c, at, :] for c in range(3)], mirror_ref, source, rows, count)
        for c, sign in enumerate((1.0, -1.0, 1.0)):
            sends[step][c] = sign * moved[:, c * LANES : (c + 1) * LANES]


def adjoint_kernel(count, rows, wall_ref, steps_ref, mirror_ref, ops_ref, gains, base, *rest):
    pieces, outs = rest[:count], rest[count : 2 * count]
    scaled, state = rest[2 * count : 2 * count + 2], rest[2 * count + 2 :]
    wall = wall_ref[0]
    ny = base.shape[1]
    for step in range(count):
        block = wall ^ step
        partner = count - 1 - block
        at = pl.ds(pl.multiple_of(partner * rows, 8), rows)
        moved = mirror_block([pieces[step][c] for c in range(3)], mirror_ref, block, rows, count)
        pair = to_groups(moved[:, :LANES], -moved[:, LANES : 2 * LANES])
        for group in range(2):
            state[group][at, :LANES] = base[group, at, :LANES] - pair[group]
            state[group][at, LANES:] = base[group, at, LANES:] - moved[:, 2 * LANES :]

    def scale(group):
        high, low = split(gains[group] * state[group][...])
        scaled[group][0:ny] = high
        scaled[group][ny : 2 * ny] = low
        scaled[group][2 * ny : 3 * ny] = high

    def multiply(group):
        state[group][...] = jnp.dot(ops_ref[group], scaled[group][...], preferred_element_type=jnp.float32)

    def advance(_, carry):
        scale(1)
        multiply(0)
        scale(0)
        multiply(1)
        return carry

    def advance_some(_, carry):
        for _ in range(STEPS_MAX // 2):
            advance(0, 0)
        return carry

    steps = jnp.minimum(steps_ref[0], STEPS_MAX)
    scale(0)
    lax.fori_loop(0, steps // (STEPS_MAX // 2), advance_some, 0)
    lax.fori_loop(0, steps % (STEPS_MAX // 2), advance, 0)
    left = left_half((rows, LANES))
    for step in range(count):
        at = pl.ds(pl.multiple_of((wall ^ step) * rows, 8), rows)
        outs[step][0], outs[step][1] = to_groups(state[0][at, :LANES], state[1][at, :LANES])
        outs[step][2] = jnp.where(left, state[0][at, LANES:], state[1][at, LANES:])


def offset_kernel(count, wall_ref, start_ref, *rest):
    parts, out_ref = rest[:-1][::-1], rest[-1]
    wall = wall_ref[0]
    for step, part in enumerate(parts):
        at = pl.ds(pl.multiple_of((wall ^ step) * LANES, LANES), LANES)
        out_ref[:, :, at] = part[...] - start_ref[:, :, at]


def combine_kernel(count, wall_ref, offset_ref, *rest):
    parts, out_ref, held, sems = rest[:count][::-1], *rest[count:]
    wall = wall_ref[0]
    copies = []
    for c in range(3):
        for step, part in enumerate(parts):
            at = pl.ds(pl.multiple_of((wall ^ step) * LANES, LANES), LANES)
            held[c, :, at] = part[c] - offset_ref[c, :, at]
        copies.append(pltpu.make_async_copy(held.at[c], out_ref.at[c], sems.at[c]))
        copies[-1].start()
    for copy in copies:
        copy.wait()


def send(part, steps, flip, shape):
    slabs, count = shape
    pairs = [(t * count + w, (t + steps) % slabs * count + (w ^ flip)) for t in range(slabs) for w in range(count)]
    return lax.ppermute(part, ("tm", "wall"), pairs)


def on_device(shape, start_state, end_state, coupling, inverse_ops, mirror_rows, slab_steps):
    slabs, count = shape
    rows = start_state.shape[2]
    ny = end_state.shape[2]
    start, end, gain = start_state[0], end_state[0], coupling[0]
    wall = lax.axis_index("wall").astype(jnp.int32).reshape(1)
    mirror_blocks = mirror_rows.reshape(count, 1, rows)
    smem = pl.BlockSpec(memory_space=pltpu.SMEM)
    vmem = pl.BlockSpec(memory_space=pltpu.VMEM)
    part = jax.ShapeDtypeStruct((3, rows, LANES), jnp.float32)
    wide = jax.ShapeDtypeStruct((2, ny, 2 * LANES), jnp.float32)
    limit = pltpu.CompilerParams(vmem_limit_bytes=24 << 20)

    outgoing = [
        lax.dynamic_slice(start, (0, 0, (wall[0] ^ step) * LANES), (3, rows, LANES)) for step in range(count)
    ]
    incoming = [send(part, -1, step, shape) for step, part in enumerate(outgoing)]

    ops, gains, base, *mirrored = pl.pallas_call(
        functools.partial(prepare_kernel, count, rows),
        out_shape=[jax.ShapeDtypeStruct((2, ny, 3 * ny), jnp.bfloat16), wide, wide] + [part] * count,
        in_specs=[smem] + [vmem] * 4,
        out_specs=[vmem] * (3 + count),
        compiler_params=limit,
        cost_estimate=pl.CostEstimate(flops=10**8, bytes_accessed=4 << 20, transcendentals=0),
        name="prepare",
    )(wall, mirror_blocks, end, gain, inverse_ops)

    mirrored, arrived = lax.optimization_barrier((mirrored, incoming[:-1]))
    incoming = arrived + incoming[-1:]
    mirrored = [send(part, 1, i, shape) for i, part in enumerate(mirrored)]

    adjoint = pl.pallas_call(
        functools.partial(adjoint_kernel, count, rows),
        out_shape=[part] * count,
        in_specs=[smem, smem] + [vmem] * (4 + count),
        out_specs=[vmem] * count,
        scratch_shapes=[pltpu.VMEM((3 * ny, 2 * LANES), jnp.bfloat16)] * 2
        + [pltpu.VMEM((ny, 2 * LANES), jnp.float32)] * 2,
        compiler_params=limit,
        cost_estimate=pl.CostEstimate(flops=4 * 10**9, bytes_accessed=4 << 20, transcendentals=0),
        name="adjoint",
    )(wall, slab_steps, mirror_blocks, ops, gains, base, *incoming)
    returned = [adjoint[0]] + [send(adjoint[step], 0, step, shape) for step in range(1, count)]

    offset = pl.pallas_call(
        functools.partial(offset_kernel, count),
        out_shape=jax.ShapeDtypeStruct(start.shape, jnp.float32),
        in_specs=[smem, vmem] + [vmem] * count,
        out_specs=vmem,
        compiler_params=limit,
        cost_estimate=pl.CostEstimate(flops=10**6, bytes_accessed=40 << 20, transcendentals=0),
        name="offset",
    )(wall, start, *mirrored[::-1])
    gradient = pl.pallas_call(
        functools.partial(combine_kernel, count),
        out_shape=jax.ShapeDtypeStruct(start.shape, jnp.float32),
        in_specs=[smem, vmem] + [vmem] * count,
        out_specs=pl.BlockSpec(memory_space=pl.ANY),
        scratch_shapes=[pltpu.VMEM(start.shape, jnp.float32), pltpu.SemaphoreType.DMA((3,))],
        compiler_params=limit,
        cost_estimate=pl.CostEstimate(flops=10**6, bytes_accessed=3 << 20, transcendentals=0),
        name="combine",
    )(wall, offset, *returned[::-1])
    return gradient[None]


def solution(mesh):
    in_specs = (
        P("tm", None, "wall", None),
        P("tm", None, None, "wall"),
        P("tm", None, None, "wall"),
        P("wall", None, None),
        P(),
        P("tm"),
    )
    out_specs = P("tm", None, "wall", None)
    shape = (mesh.shape["tm"], mesh.shape["wall"])
    return jax.shard_map(
        functools.partial(on_device, shape),
        mesh=mesh,
        in_specs=in_specs,
        out_specs=out_specs,
        check_vma=False,
    )
```

```python
import functools

import jax
import jax.numpy as jnp
from jax import lax
from jax.experimental import pallas as pl
from jax.experimental.pallas import tpu as pltpu
from jax.sharding import PartitionSpec as P

STEPS_MAX = 8
LANES = 128
HALF = LANES // 2


def split(values):
    high = values.astype(jnp.bfloat16)
    low = (values - high.astype(jnp.float32)).astype(jnp.bfloat16)
    return high, low


def swap_halves(values):
    return pltpu.roll(values, HALF, 1)


def left_half(shape):
    return lax.broadcasted_iota(jnp.int32, shape, 1) < HALF


def to_groups(first, second):
    left = left_half(first.shape)
    return jnp.where(left, first, swap_halves(second)), jnp.where(left, swap_halves(first), second)


def mirror_block(pieces, mirror_ref, block, rows, count):
    partner = count - 1 - block
    target = mirror_ref[block] - partner * rows
    lane = lax.broadcasted_iota(jnp.int32, (rows, rows), 0)
    one_hot = (lane == target).astype(jnp.bfloat16)
    values = jnp.concatenate(pieces, axis=1)
    high, low = split(values)
    return jnp.dot(
        jnp.concatenate([one_hot, one_hot], axis=1),
        jnp.concatenate([high, low], axis=0),
        preferred_element_type=jnp.float32,
    )


def prepare_kernel(count, rows, wall_ref, mirror_ref, end_ref, coupling_ref, ops_ref, ops_out, gains, base, *sends):
    wall = wall_ref[0]
    ny = ops_ref.shape[1]
    left = left_half((ny, LANES))
    for group in range(2):
        high, low = split(ops_ref[group])
        ops_out[group, :, 0:ny] = high
        ops_out[group, :, ny : 2 * ny] = high
        ops_out[group, :, 2 * ny : 3 * ny] = low
    gains[0, :, :LANES], gains[1, :, :LANES] = to_groups(coupling_ref[0], coupling_ref[1])
    gains[0, :, LANES:] = jnp.where(left, coupling_ref[2], 0.0)
    gains[1, :, LANES:] = jnp.where(left, 0.0, coupling_ref[2])
    base[0, :, :LANES], base[1, :, :LANES] = to_groups(end_ref[0], end_ref[1])
    base[0, :, LANES:] = end_ref[2]
    base[1, :, LANES:] = end_ref[2]
    for step in range(count):
        source = count - 1 - (wall ^ step)
        at = pl.ds(pl.multiple_of(source * rows, 8), rows)
        moved = mirror_block([end_ref[c, at, :] for c in range(3)], mirror_ref, source, rows, count)
        for c, sign in enumerate((1.0, -1.0, 1.0)):
            sends[step][c] = sign * moved[:, c * LANES : (c + 1) * LANES]


def adjoint_kernel(count, rows, wall_ref, steps_ref, mirror_ref, ops_ref, gains, base, *rest):
    pieces, outs = rest[:count], rest[count : 2 * count]
    scaled, state = rest[2 * count : 2 * count + 2], rest[2 * count + 2 :]
    wall = wall_ref[0]
    ny = base.shape[1]
    for step in range(count):
        block = wall ^ step
        partner = count - 1 - block
        at = pl.ds(pl.multiple_of(partner * rows, 8), rows)
        moved = mirror_block([pieces[step][c] for c in range(3)], mirror_ref, block, rows, count)
        pair = to_groups(moved[:, :LANES], -moved[:, LANES : 2 * LANES])
        for group in range(2):
            state[group][at, :LANES] = base[group, at, :LANES] - pair[group]
            state[group][at, LANES:] = base[group, at, LANES:] - moved[:, 2 * LANES :]

    def scale(group):
        high, low = split(gains[group] * state[group][...])
        scaled[group][0:ny] = high
        scaled[group][ny : 2 * ny] = low
        scaled[group][2 * ny : 3 * ny] = high

    def multiply(group):
        state[group][...] = jnp.dot(ops_ref[group], scaled[group][...], preferred_element_type=jnp.float32)

    def advance(_, carry):
        scale(1)
        multiply(0)
        scale(0)
        multiply(1)
        return carry

    def advance_some(_, carry):
        for _ in range(STEPS_MAX // 2):
            advance(0, 0)
        return carry

    steps = jnp.minimum(steps_ref[0], STEPS_MAX)
    scale(0)
    lax.fori_loop(0, steps // (STEPS_MAX // 2), advance_some, 0)
    lax.fori_loop(0, steps % (STEPS_MAX // 2), advance, 0)
    left = left_half((rows, LANES))
    for step in range(count):
        at = pl.ds(pl.multiple_of((wall ^ step) * rows, 8), rows)
        outs[step][0], outs[step][1] = to_groups(state[0][at, :LANES], state[1][at, :LANES])
        outs[step][2] = jnp.where(left, state[0][at, LANES:], state[1][at, LANES:])


def offset_kernel(count, wall_ref, start_ref, *rest):
    parts, out_ref = rest[:-1][::-1], rest[-1]
    wall = wall_ref[0]
    for step, part in enumerate(parts):
        at = pl.ds(pl.multiple_of((wall ^ step) * LANES, LANES), LANES)
        out_ref[:, :, at] = part[...] - start_ref[:, :, at]


def combine_kernel(count, wall_ref, offset_ref, *rest):
    parts, out_ref, held, sems = rest[:count][::-1], *rest[count:]
    wall = wall_ref[0]
    copies = []
    for c in range(3):
        for step, part in enumerate(parts):
            at = pl.ds(pl.multiple_of((wall ^ step) * LANES, LANES), LANES)
            held[c, :, at] = part[c] - offset_ref[c, :, at]
        copies.append(pltpu.make_async_copy(held.at[c], out_ref.at[c], sems.at[c]))
        copies[-1].start()
    for copy in copies:
        copy.wait()


def send(part, steps, flip, shape):
    slabs, count = shape
    pairs = [(t * count + w, (t + steps) % slabs * count + (w ^ flip)) for t in range(slabs) for w in range(count)]
    return lax.ppermute(part, ("tm", "wall"), pairs)


def on_device(shape, start_state, end_state, coupling, inverse_ops, mirror_rows, slab_steps):
    slabs, count = shape
    rows = start_state.shape[2]
    ny = end_state.shape[2]
    start, end, gain = start_state[0], end_state[0], coupling[0]
    wall = lax.axis_index("wall").astype(jnp.int32).reshape(1)
    mirror_blocks = mirror_rows.reshape(count, 1, rows)
    smem = pl.BlockSpec(memory_space=pltpu.SMEM)
    vmem = pl.BlockSpec(memory_space=pltpu.VMEM)
    part = jax.ShapeDtypeStruct((3, rows, LANES), jnp.float32)
    wide = jax.ShapeDtypeStruct((2, ny, 2 * LANES), jnp.float32)
    limit = pltpu.CompilerParams(vmem_limit_bytes=24 << 20)

    outgoing = [
        lax.dynamic_slice(start, (0, 0, (wall[0] ^ step) * LANES), (3, rows, LANES)) for step in range(count)
    ]
    incoming = [send(part, -1, step, shape) for step, part in enumerate(outgoing)]

    end, incoming[:2] = lax.optimization_barrier((end, incoming[:2]))
    ops, gains, base, *mirrored = pl.pallas_call(
        functools.partial(prepare_kernel, count, rows),
        out_shape=[jax.ShapeDtypeStruct((2, ny, 3 * ny), jnp.bfloat16), wide, wide] + [part] * count,
        in_specs=[smem] + [vmem] * 4,
        out_specs=[vmem] * (3 + count),
        compiler_params=limit,
        cost_estimate=pl.CostEstimate(flops=10**8, bytes_accessed=4 << 20, transcendentals=0),
        name="prepare",
    )(wall, mirror_blocks, end, gain, inverse_ops)

    mirrored = [send(part, 1, i, shape) for i, part in enumerate(mirrored)]

    adjoint = pl.pallas_call(
        functools.partial(adjoint_kernel, count, rows),
        out_shape=[part] * count,
        in_specs=[smem, smem] + [vmem] * (4 + count),
        out_specs=[vmem] * count,
        scratch_shapes=[pltpu.VMEM((3 * ny, 2 * LANES), jnp.bfloat16)] * 2
        + [pltpu.VMEM((ny, 2 * LANES), jnp.float32)] * 2,
        compiler_params=limit,
        cost_estimate=pl.CostEstimate(flops=4 * 10**9, bytes_accessed=4 << 20, transcendentals=0),
        name="adjoint",
    )(wall, slab_steps, mirror_blocks, ops, gains, base, *incoming)
    returned = [adjoint[0]] + [send(adjoint[step], 0, step, shape) for step in range(1, count)]

    offset = pl.pallas_call(
        functools.partial(offset_kernel, count),
        out_shape=jax.ShapeDtypeStruct(start.shape, jnp.float32),
        in_specs=[smem, vmem] + [vmem] * count,
        out_specs=vmem,
        compiler_params=limit,
        cost_estimate=pl.CostEstimate(flops=10**6, bytes_accessed=40 << 20, transcendentals=0),
        name="offset",
    )(wall, start, *mirrored[::-1])
    gradient = pl.pallas_call(
        functools.partial(combine_kernel, count),
        out_shape=jax.ShapeDtypeStruct(start.shape, jnp.float32),
        in_specs=[smem, vmem] + [vmem] * count,
        out_specs=pl.BlockSpec(memory_space=pl.ANY),
        scratch_shapes=[pltpu.VMEM(start.shape, jnp.float32), pltpu.SemaphoreType.DMA((3,))],
        compiler_params=limit,
        cost_estimate=pl.CostEstimate(flops=10**6, bytes_accessed=3 << 20, transcendentals=0),
        name="combine",
    )(wall, offset, *returned[::-1])
    return gradient[None]


def solution(mesh):
    in_specs = (
        P("tm", None, "wall", None),
        P("tm", None, None, "wall"),
        P("tm", None, None, "wall"),
        P("wall", None, None),
        P(),
        P("tm"),
    )
    out_specs = P("tm", None, "wall", None)
    shape = (mesh.shape["tm"], mesh.shape["wall"])
    return jax.shard_map(
        functools.partial(on_device, shape),
        mesh=mesh,
        in_specs=in_specs,
        out_specs=out_specs,
        check_vma=False,
    )
```

```python
import functools

import jax
import jax.numpy as jnp
from jax import lax
from jax.experimental import pallas as pl
from jax.experimental.pallas import tpu as pltpu
from jax.sharding import PartitionSpec as P

STEPS_MAX = 8
LANES = 128
HALF = LANES // 2


def return_order(count):
    return [*range(count // 2, count), *reversed(range(count // 2))]


def unorder(order, parts):
    return [parts[order.index(step)] for step in range(len(order))]


def split(values):
    high = values.astype(jnp.bfloat16)
    low = (values - high.astype(jnp.float32)).astype(jnp.bfloat16)
    return high, low


def swap_halves(values):
    return pltpu.roll(values, HALF, 1)


def left_half(shape):
    return lax.broadcasted_iota(jnp.int32, shape, 1) < HALF


def to_groups(first, second):
    left = left_half(first.shape)
    return jnp.where(left, first, swap_halves(second)), jnp.where(left, swap_halves(first), second)


def mirror_block(pieces, mirror_ref, block, rows, count):
    partner = count - 1 - block
    target = mirror_ref[block] - partner * rows
    lane = lax.broadcasted_iota(jnp.int32, (rows, rows), 0)
    one_hot = (lane == target).astype(jnp.bfloat16)
    values = jnp.concatenate(pieces, axis=1)
    high, low = split(values)
    return jnp.dot(
        jnp.concatenate([one_hot, one_hot], axis=1),
        jnp.concatenate([high, low], axis=0),
        preferred_element_type=jnp.float32,
    )


def prepare_kernel(count, rows, wall_ref, mirror_ref, end_ref, coupling_ref, ops_ref, ops_out, gains, base, *sends):
    wall = wall_ref[0]
    ny = ops_ref.shape[1]
    left = left_half((ny, LANES))
    for group in range(2):
        high, low = split(ops_ref[group])
        ops_out[group, :, 0:ny] = high
        ops_out[group, :, ny : 2 * ny] = high
        ops_out[group, :, 2 * ny : 3 * ny] = low
    gains[0, :, :LANES], gains[1, :, :LANES] = to_groups(coupling_ref[0], coupling_ref[1])
    gains[0, :, LANES:] = jnp.where(left, coupling_ref[2], 0.0)
    gains[1, :, LANES:] = jnp.where(left, 0.0, coupling_ref[2])
    base[0, :, :LANES], base[1, :, :LANES] = to_groups(end_ref[0], end_ref[1])
    base[0, :, LANES:] = end_ref[2]
    base[1, :, LANES:] = end_ref[2]
    for step in range(count):
        source = count - 1 - (wall ^ step)
        at = pl.ds(pl.multiple_of(source * rows, 8), rows)
        moved = mirror_block([end_ref[c, at, :] for c in range(3)], mirror_ref, source, rows, count)
        for c, sign in enumerate((1.0, -1.0, 1.0)):
            sends[step][c] = sign * moved[:, c * LANES : (c + 1) * LANES]


def adjoint_kernel(count, rows, wall_ref, steps_ref, mirror_ref, ops_ref, gains, base, *rest):
    pieces, outs = rest[:count], rest[count : 2 * count]
    scaled, state = rest[2 * count : 2 * count + 2], rest[2 * count + 2 :]
    wall = wall_ref[0]
    ny = base.shape[1]
    for step in range(count):
        block = wall ^ step
        partner = count - 1 - block
        at = pl.ds(pl.multiple_of(partner * rows, 8), rows)
        moved = mirror_block([pieces[step][c] for c in range(3)], mirror_ref, block, rows, count)
        pair = to_groups(moved[:, :LANES], -moved[:, LANES : 2 * LANES])
        for group in range(2):
            state[group][at, :LANES] = base[group, at, :LANES] - pair[group]
            state[group][at, LANES:] = base[group, at, LANES:] - moved[:, 2 * LANES :]

    def scale(group):
        high, low = split(gains[group] * state[group][...])
        scaled[group][0:ny] = high
        scaled[group][ny : 2 * ny] = low
        scaled[group][2 * ny : 3 * ny] = high

    def multiply(group):
        state[group][...] = jnp.dot(ops_ref[group], scaled[group][...], preferred_element_type=jnp.float32)

    def advance(_, carry):
        scale(1)
        multiply(0)
        scale(0)
        multiply(1)
        return carry

    def advance_some(_, carry):
        for _ in range(STEPS_MAX // 2):
            advance(0, 0)
        return carry

    steps = jnp.minimum(steps_ref[0], STEPS_MAX)
    scale(0)
    lax.fori_loop(0, steps // (STEPS_MAX // 2), advance_some, 0)
    lax.fori_loop(0, steps % (STEPS_MAX // 2), advance, 0)
    left = left_half((rows, LANES))
    for step in range(count):
        at = pl.ds(pl.multiple_of((wall ^ step) * rows, 8), rows)
        outs[step][0], outs[step][1] = to_groups(state[0][at, :LANES], state[1][at, :LANES])
        outs[step][2] = jnp.where(left, state[0][at, LANES:], state[1][at, LANES:])


def offset_kernel(count, wall_ref, start_ref, *rest):
    parts, out_ref = rest[:-1][::-1], rest[-1]
    wall = wall_ref[0]
    for step, part in enumerate(parts):
        at = pl.ds(pl.multiple_of((wall ^ step) * LANES, LANES), LANES)
        out_ref[:, :, at] = part[...] - start_ref[:, :, at]


def combine_kernel(count, wall_ref, offset_ref, *rest):
    parts, out_ref, held, sems = unorder(return_order(count), rest[:count]), *rest[count:]
    wall = wall_ref[0]
    copies = []
    for c in range(3):
        for step, part in enumerate(parts):
            at = pl.ds(pl.multiple_of((wall ^ step) * LANES, LANES), LANES)
            held[c, :, at] = part[c] - offset_ref[c, :, at]
        copies.append(pltpu.make_async_copy(held.at[c], out_ref.at[c], sems.at[c]))
        copies[-1].start()
    for copy in copies:
        copy.wait()


def send(part, steps, flip, shape):
    slabs, count = shape
    pairs = [(t * count + w, (t + steps) % slabs * count + (w ^ flip)) for t in range(slabs) for w in range(count)]
    return lax.ppermute(part, ("tm", "wall"), pairs)


def on_device(shape, start_state, end_state, coupling, inverse_ops, mirror_rows, slab_steps):
    slabs, count = shape
    rows = start_state.shape[2]
    ny = end_state.shape[2]
    start, end, gain = start_state[0], end_state[0], coupling[0]
    wall = lax.axis_index("wall").astype(jnp.int32).reshape(1)
    mirror_blocks = mirror_rows.reshape(count, 1, rows)
    smem = pl.BlockSpec(memory_space=pltpu.SMEM)
    vmem = pl.BlockSpec(memory_space=pltpu.VMEM)
    part = jax.ShapeDtypeStruct((3, rows, LANES), jnp.float32)
    wide = jax.ShapeDtypeStruct((2, ny, 2 * LANES), jnp.float32)
    limit = pltpu.CompilerParams(vmem_limit_bytes=24 << 20)

    outgoing = [
        lax.dynamic_slice(start, (0, 0, (wall[0] ^ step) * LANES), (3, rows, LANES)) for step in range(count)
    ]
    incoming = [send(part, -1, step, shape) for step, part in enumerate(outgoing)]

    inverse_ops, incoming[:2] = lax.optimization_barrier((inverse_ops, incoming[:2]))
    ops, gains, base, *mirrored = pl.pallas_call(
        functools.partial(prepare_kernel, count, rows),
        out_shape=[jax.ShapeDtypeStruct((2, ny, 3 * ny), jnp.bfloat16), wide, wide] + [part] * count,
        in_specs=[smem] + [vmem] * 4,
        out_specs=[vmem] * (3 + count),
        compiler_params=limit,
        cost_estimate=pl.CostEstimate(flops=10**8, bytes_accessed=4 << 20, transcendentals=0),
        name="prepare",
    )(wall, mirror_blocks, end, gain, inverse_ops)

    mirrored = mirrored[:1] + [send(part, 1, i, shape) for i, part in enumerate(mirrored) if i]
    mirrored[0], mirrored[-1] = lax.optimization_barrier((mirrored[0], mirrored[-1]))
    mirrored[0] = send(mirrored[0], 1, 0, shape)

    adjoint = pl.pallas_call(
        functools.partial(adjoint_kernel, count, rows),
        out_shape=[part] * count,
        in_specs=[smem, smem] + [vmem] * (4 + count),
        out_specs=[vmem] * count,
        scratch_shapes=[pltpu.VMEM((3 * ny, 2 * LANES), jnp.bfloat16)] * 2
        + [pltpu.VMEM((ny, 2 * LANES), jnp.float32)] * 2,
        compiler_params=limit,
        cost_estimate=pl.CostEstimate(flops=4 * 10**9, bytes_accessed=4 << 20, transcendentals=0),
        name="adjoint",
    )(wall, slab_steps, mirror_blocks, ops, gains, base, *incoming)
    returned = [adjoint[0]] + [send(adjoint[step], 0, step, shape) for step in range(1, count)]

    offset = pl.pallas_call(
        functools.partial(offset_kernel, count),
        out_shape=jax.ShapeDtypeStruct(start.shape, jnp.float32),
        in_specs=[smem, vmem] + [vmem] * count,
        out_specs=vmem,
        compiler_params=limit,
        cost_estimate=pl.CostEstimate(flops=10**6, bytes_accessed=40 << 20, transcendentals=0),
        name="offset",
    )(wall, start, *mirrored[::-1])
    gradient = pl.pallas_call(
        functools.partial(combine_kernel, count),
        out_shape=jax.ShapeDtypeStruct(start.shape, jnp.float32),
        in_specs=[smem, vmem] + [vmem] * count,
        out_specs=pl.BlockSpec(memory_space=pl.ANY),
        scratch_shapes=[pltpu.VMEM(start.shape, jnp.float32), pltpu.SemaphoreType.DMA((3,))],
        compiler_params=limit,
        cost_estimate=pl.CostEstimate(flops=10**6, bytes_accessed=3 << 20, transcendentals=0),
        name="combine",
    )(wall, offset, *[returned[step] for step in return_order(count)])
    return gradient[None]


def solution(mesh):
    in_specs = (
        P("tm", None, "wall", None),
        P("tm", None, None, "wall"),
        P("tm", None, None, "wall"),
        P("wall", None, None),
        P(),
        P("tm"),
    )
    out_specs = P("tm", None, "wall", None)
    shape = (mesh.shape["tm"], mesh.shape["wall"])
    return jax.shard_map(
        functools.partial(on_device, shape),
        mesh=mesh,
        in_specs=in_specs,
        out_specs=out_specs,
        check_vma=False,
    )
```

```python
import functools

import jax
import jax.numpy as jnp
from jax import lax
from jax.experimental import pallas as pl
from jax.experimental.pallas import tpu as pltpu
from jax.sharding import PartitionSpec as P

STEPS_MAX = 8
LANES = 128
HALF = LANES // 2


def return_order(count):
    return [*range(count // 2, count), *reversed(range(count // 2))]


def unorder(order, parts):
    return [parts[order.index(step)] for step in range(len(order))]


def split(values):
    high = values.astype(jnp.bfloat16)
    low = (values - high.astype(jnp.float32)).astype(jnp.bfloat16)
    return high, low


def swap_halves(values):
    return pltpu.roll(values, HALF, 1)


def left_half(shape):
    return lax.broadcasted_iota(jnp.int32, shape, 1) < HALF


def to_groups(first, second):
    left = left_half(first.shape)
    return jnp.where(left, first, swap_halves(second)), jnp.where(left, swap_halves(first), second)


def mirror_block(pieces, mirror_ref, block, rows, count):
    partner = count - 1 - block
    target = mirror_ref[block] - partner * rows
    lane = lax.broadcasted_iota(jnp.int32, (rows, rows), 0)
    one_hot = (lane == target).astype(jnp.bfloat16)
    values = jnp.concatenate(pieces, axis=1)
    high, low = split(values)
    return jnp.dot(
        jnp.concatenate([one_hot, one_hot], axis=1),
        jnp.concatenate([high, low], axis=0),
        preferred_element_type=jnp.float32,
    )


def prepare_kernel(count, rows, wall_ref, mirror_ref, end_ref, coupling_ref, ops_ref, ops_out, gains, base, *sends):
    wall = wall_ref[0]
    ny = ops_ref.shape[1]
    left = left_half((ny, LANES))
    for group in range(2):
        high, low = split(ops_ref[group])
        ops_out[group, :, 0:ny] = high
        ops_out[group, :, ny : 2 * ny] = high
        ops_out[group, :, 2 * ny : 3 * ny] = low
    gains[0, :, :LANES], gains[1, :, :LANES] = to_groups(coupling_ref[0], coupling_ref[1])
    gains[0, :, LANES:] = jnp.where(left, coupling_ref[2], 0.0)
    gains[1, :, LANES:] = jnp.where(left, 0.0, coupling_ref[2])
    base[0, :, :LANES], base[1, :, :LANES] = to_groups(end_ref[0], end_ref[1])
    base[0, :, LANES:] = end_ref[2]
    base[1, :, LANES:] = end_ref[2]
    for step in range(count):
        source = count - 1 - (wall ^ step)
        at = pl.ds(pl.multiple_of(source * rows, 8), rows)
        moved = mirror_block([end_ref[c, at, :] for c in range(3)], mirror_ref, source, rows, count)
        for c, sign in enumerate((1.0, -1.0, 1.0)):
            sends[step][c] = sign * moved[:, c * LANES : (c + 1) * LANES]


def adjoint_kernel(count, rows, wall_ref, steps_ref, mirror_ref, ops_ref, gains, base, *rest):
    pieces, outs = rest[:count], rest[count : 2 * count]
    scaled, state = rest[2 * count : 2 * count + 2], rest[2 * count + 2 :]
    wall = wall_ref[0]
    ny = base.shape[1]
    for step in range(count):
        block = wall ^ step
        partner = count - 1 - block
        at = pl.ds(pl.multiple_of(partner * rows, 8), rows)
        moved = mirror_block([pieces[step][c] for c in range(3)], mirror_ref, block, rows, count)
        pair = to_groups(moved[:, :LANES], -moved[:, LANES : 2 * LANES])
        for group in range(2):
            state[group][at, :LANES] = base[group, at, :LANES] - pair[group]
            state[group][at, LANES:] = base[group, at, LANES:] - moved[:, 2 * LANES :]

    def scale(group):
        high, low = split(gains[group] * state[group][...])
        scaled[group][0:ny] = high
        scaled[group][ny : 2 * ny] = low
        scaled[group][2 * ny : 3 * ny] = high

    def multiply(group):
        for at in (pl.ds(0, ny // 2), pl.ds(ny // 2, ny // 2)):
            state[group][at, :] = jnp.dot(ops_ref[group, at, :], scaled[group][...], preferred_element_type=jnp.float32)

    def advance(_, carry):
        scale(1)
        multiply(0)
        scale(0)
        multiply(1)
        return carry

    def advance_most(_, carry):
        for _ in range(STEPS_MAX):
            advance(0, 0)
        return carry

    steps = jnp.minimum(steps_ref[0], STEPS_MAX)
    scale(0)
    lax.fori_loop(0, steps // STEPS_MAX, advance_most, 0)
    lax.fori_loop(0, steps % STEPS_MAX, advance, 0)
    left = left_half((rows, LANES))
    for step in range(count):
        at = pl.ds(pl.multiple_of((wall ^ step) * rows, 8), rows)
        outs[step][0], outs[step][1] = to_groups(state[0][at, :LANES], state[1][at, :LANES])
        outs[step][2] = jnp.where(left, state[0][at, LANES:], state[1][at, LANES:])


def offset_kernel(count, wall_ref, start_ref, *rest):
    parts, out_ref = rest[:-1][::-1], rest[-1]
    wall = wall_ref[0]
    for step, part in enumerate(parts):
        at = pl.ds(pl.multiple_of((wall ^ step) * LANES, LANES), LANES)
        out_ref[:, :, at] = part[...] - start_ref[:, :, at]


def combine_kernel(count, wall_ref, offset_ref, *rest):
    parts, out_ref, held, sems = unorder(return_order(count), rest[:count]), *rest[count:]
    wall = wall_ref[0]
    copies = []
    for c in range(3):
        for step, part in enumerate(parts):
            at = pl.ds(pl.multiple_of((wall ^ step) * LANES, LANES), LANES)
            held[c, :, at] = part[c] - offset_ref[c, :, at]
        copies.append(pltpu.make_async_copy(held.at[c], out_ref.at[c], sems.at[c]))
        copies[-1].start()
    for copy in copies:
        copy.wait()


def send(part, steps, flip, shape):
    slabs, count = shape
    pairs = [(t * count + w, (t + steps) % slabs * count + (w ^ flip)) for t in range(slabs) for w in range(count)]
    return lax.ppermute(part, ("tm", "wall"), pairs)


def on_device(shape, start_state, end_state, coupling, inverse_ops, mirror_rows, slab_steps):
    slabs, count = shape
    rows = start_state.shape[2]
    ny = end_state.shape[2]
    start, end, gain = start_state[0], end_state[0], coupling[0]
    wall = lax.axis_index("wall").astype(jnp.int32).reshape(1)
    mirror_blocks = mirror_rows.reshape(count, 1, rows)
    smem = pl.BlockSpec(memory_space=pltpu.SMEM)
    vmem = pl.BlockSpec(memory_space=pltpu.VMEM)
    part = jax.ShapeDtypeStruct((3, rows, LANES), jnp.float32)
    wide = jax.ShapeDtypeStruct((2, ny, 2 * LANES), jnp.float32)
    limit = pltpu.CompilerParams(vmem_limit_bytes=24 << 20)

    outgoing = [
        lax.dynamic_slice(start, (0, 0, (wall[0] ^ step) * LANES), (3, rows, LANES)) for step in range(count)
    ]
    incoming = [send(part, -1, step, shape) for step, part in enumerate(outgoing)]

    inverse_ops, incoming[:2] = lax.optimization_barrier((inverse_ops, incoming[:2]))
    ops, gains, base, *mirrored = pl.pallas_call(
        functools.partial(prepare_kernel, count, rows),
        out_shape=[jax.ShapeDtypeStruct((2, ny, 3 * ny), jnp.bfloat16), wide, wide] + [part] * count,
        in_specs=[smem] + [vmem] * 4,
        out_specs=[vmem] * (3 + count),
        compiler_params=limit,
        cost_estimate=pl.CostEstimate(flops=10**8, bytes_accessed=4 << 20, transcendentals=0),
        name="prepare",
    )(wall, mirror_blocks, end, gain, inverse_ops)

    mirrored = mirrored[:1] + [send(part, 1, i, shape) for i, part in enumerate(mirrored) if i]
    mirrored[0], mirrored[-1] = lax.optimization_barrier((mirrored[0], mirrored[-1]))
    mirrored[0] = send(mirrored[0], 1, 0, shape)

    adjoint = pl.pallas_call(
        functools.partial(adjoint_kernel, count, rows),
        out_shape=[part] * count,
        in_specs=[smem, smem] + [vmem] * (4 + count),
        out_specs=[vmem] * count,
        scratch_shapes=[pltpu.VMEM((3 * ny, 2 * LANES), jnp.bfloat16)] * 2
        + [pltpu.VMEM((ny, 2 * LANES), jnp.float32)] * 2,
        compiler_params=limit,
        cost_estimate=pl.CostEstimate(flops=4 * 10**9, bytes_accessed=4 << 20, transcendentals=0),
        name="adjoint",
    )(wall, slab_steps, mirror_blocks, ops, gains, base, *incoming)
    returned = [adjoint[0]] + [send(adjoint[step], 0, step, shape) for step in range(1, count)]

    offset = pl.pallas_call(
        functools.partial(offset_kernel, count),
        out_shape=jax.ShapeDtypeStruct(start.shape, jnp.float32),
        in_specs=[smem, vmem] + [vmem] * count,
        out_specs=vmem,
        compiler_params=limit,
        cost_estimate=pl.CostEstimate(flops=10**6, bytes_accessed=40 << 20, transcendentals=0),
        name="offset",
    )(wall, start, *mirrored[::-1])
    gradient = pl.pallas_call(
        functools.partial(combine_kernel, count),
        out_shape=jax.ShapeDtypeStruct(start.shape, jnp.float32),
        in_specs=[smem, vmem] + [vmem] * count,
        out_specs=pl.BlockSpec(memory_space=pl.ANY),
        scratch_shapes=[pltpu.VMEM(start.shape, jnp.float32), pltpu.SemaphoreType.DMA((3,))],
        compiler_params=limit,
        cost_estimate=pl.CostEstimate(flops=10**6, bytes_accessed=3 << 20, transcendentals=0),
        name="combine",
    )(wall, offset, *[returned[step] for step in return_order(count)])
    return gradient[None]


def solution(mesh):
    in_specs = (
        P("tm", None, "wall", None),
        P("tm", None, None, "wall"),
        P("tm", None, None, "wall"),
        P("wall", None, None),
        P(),
        P("tm"),
    )
    out_specs = P("tm", None, "wall", None)
    shape = (mesh.shape["tm"], mesh.shape["wall"])
    return jax.shard_map(
        functools.partial(on_device, shape),
        mesh=mesh,
        in_specs=in_specs,
        out_specs=out_specs,
        check_vma=False,
    )
```

```python
import functools

import jax
import jax.numpy as jnp
from jax import lax
from jax.experimental import pallas as pl
from jax.experimental.pallas import tpu as pltpu
from jax.sharding import PartitionSpec as P

STEPS_MAX = 8
LANES = 128
HALF = LANES // 2


def return_order(count):
    return [*range(count // 2, count), *reversed(range(count // 2))]


def unorder(order, parts):
    return [parts[order.index(step)] for step in range(len(order))]


def split(values):
    high = values.astype(jnp.bfloat16)
    low = (values - high.astype(jnp.float32)).astype(jnp.bfloat16)
    return high, low


def swap_halves(values):
    return pltpu.roll(values, HALF, 1)


def left_half(shape):
    return lax.broadcasted_iota(jnp.int32, shape, 1) < HALF


def to_groups(first, second):
    left = left_half(first.shape)
    return jnp.where(left, first, swap_halves(second)), jnp.where(left, swap_halves(first), second)


def mirror_block(pieces, mirror_ref, block, rows, count):
    partner = count - 1 - block
    target = mirror_ref[block] - partner * rows
    lane = lax.broadcasted_iota(jnp.int32, (rows, rows), 0)
    one_hot = (lane == target).astype(jnp.bfloat16)
    values = jnp.concatenate(pieces, axis=1)
    high, low = split(values)
    return jnp.dot(
        jnp.concatenate([one_hot, one_hot], axis=1),
        jnp.concatenate([high, low], axis=0),
        preferred_element_type=jnp.float32,
    )


def prepare_kernel(count, rows, wall_ref, mirror_ref, end_ref, coupling_ref, ops_ref, ops_out, gains, base, *sends):
    wall = wall_ref[0]
    ny = ops_ref.shape[1]
    left = left_half((ny, LANES))
    for group in range(2):
        high, low = split(ops_ref[group])
        ops_out[group, :, 0:ny] = high
        ops_out[group, :, ny : 2 * ny] = high
        ops_out[group, :, 2 * ny : 3 * ny] = low
    gains[0, :, :LANES], gains[1, :, :LANES] = to_groups(coupling_ref[0], coupling_ref[1])
    gains[0, :, LANES:] = jnp.where(left, coupling_ref[2], 0.0)
    gains[1, :, LANES:] = jnp.where(left, 0.0, coupling_ref[2])
    base[0, :, :LANES], base[1, :, :LANES] = to_groups(end_ref[0], end_ref[1])
    base[0, :, LANES:] = end_ref[2]
    base[1, :, LANES:] = end_ref[2]
    for step in range(count):
        source = count - 1 - (wall ^ step)
        at = pl.ds(pl.multiple_of(source * rows, 8), rows)
        moved = mirror_block([end_ref[c, at, :] for c in range(3)], mirror_ref, source, rows, count)
        for c, sign in enumerate((1.0, -1.0, 1.0)):
            sends[step][c] = sign * moved[:, c * LANES : (c + 1) * LANES]


def adjoint_kernel(count, rows, wall_ref, steps_ref, mirror_ref, ops_ref, gains, base, *rest):
    pieces, outs = rest[:count], rest[count : 2 * count]
    scaled, state = rest[2 * count : 2 * count + 2], rest[2 * count + 2 :]
    wall = wall_ref[0]
    ny = base.shape[1]
    for step in range(count):
        block = wall ^ step
        partner = count - 1 - block
        at = pl.ds(pl.multiple_of(partner * rows, 8), rows)
        moved = mirror_block([pieces[step][c] for c in range(3)], mirror_ref, block, rows, count)
        pair = to_groups(moved[:, :LANES], -moved[:, LANES : 2 * LANES])
        for group in range(2):
            state[group][at, :LANES] = base[group, at, :LANES] - pair[group]
            state[group][at, LANES:] = base[group, at, LANES:] - moved[:, 2 * LANES :]

    def scale(group):
        high, low = split(gains[group] * state[group][...])
        scaled[group][0:ny] = high
        scaled[group][ny : 2 * ny] = low
        scaled[group][2 * ny : 3 * ny] = high

    def multiply(group):
        for at in (pl.ds(0, ny // 2), pl.ds(ny // 2, ny // 2)):
            state[group][at, :] = jnp.dot(ops_ref[group, at, :], scaled[group][...], preferred_element_type=jnp.float32)

    def advance(_, carry):
        scale(1)
        multiply(0)
        scale(0)
        multiply(1)
        return carry

    def advance_most(_, carry):
        for _ in range(STEPS_MAX):
            advance(0, 0)
        return carry

    steps = jnp.minimum(steps_ref[0], STEPS_MAX)
    scale(0)
    lax.fori_loop(0, steps // STEPS_MAX, advance_most, 0)
    lax.fori_loop(0, steps % STEPS_MAX, advance, 0)
    left = left_half((rows, LANES))
    for step in range(count):
        at = pl.ds(pl.multiple_of((wall ^ step) * rows, 8), rows)
        outs[step][0], outs[step][1] = to_groups(state[0][at, :LANES], state[1][at, :LANES])
        outs[step][2] = jnp.where(left, state[0][at, LANES:], state[1][at, LANES:])


def offset_kernel(count, wall_ref, start_ref, *rest):
    parts, out_ref = rest[:-1][::-1], rest[-1]
    wall = wall_ref[0]
    for step, part in enumerate(parts):
        at = pl.ds(pl.multiple_of((wall ^ step) * LANES, LANES), LANES)
        out_ref[:, :, at] = part[...] - start_ref[:, :, at]


def combine_kernel(count, wall_ref, offset_ref, *rest):
    parts, out_ref, held, sems = unorder(return_order(count), rest[:count]), *rest[count:]
    wall = wall_ref[0]
    copies = []
    for c in range(3):
        for step, part in enumerate(parts):
            at = pl.ds(pl.multiple_of((wall ^ step) * LANES, LANES), LANES)
            held[c, :, at] = part[c] - offset_ref[c, :, at]
        copies.append(pltpu.make_async_copy(held.at[c], out_ref.at[c], sems.at[c]))
        copies[-1].start()
    for copy in copies:
        copy.wait()


def send(part, steps, flip, shape):
    slabs, count = shape
    pairs = [(t * count + w, (t + steps) % slabs * count + (w ^ flip)) for t in range(slabs) for w in range(count)]
    return lax.ppermute(part, ("tm", "wall"), pairs)


def on_device(shape, start_state, end_state, coupling, inverse_ops, mirror_rows, slab_steps):
    slabs, count = shape
    rows = start_state.shape[2]
    ny = end_state.shape[2]
    start, end, gain = start_state[0], end_state[0], coupling[0]
    wall = lax.axis_index("wall").astype(jnp.int32).reshape(1)
    mirror_blocks = mirror_rows.reshape(count, 1, rows)
    smem = pl.BlockSpec(memory_space=pltpu.SMEM)
    vmem = pl.BlockSpec(memory_space=pltpu.VMEM)
    part = jax.ShapeDtypeStruct((3, rows, LANES), jnp.float32)
    wide = jax.ShapeDtypeStruct((2, ny, 2 * LANES), jnp.float32)
    limit = pltpu.CompilerParams(vmem_limit_bytes=24 << 20)

    outgoing = [
        lax.dynamic_slice(start, (0, 0, (wall[0] ^ step) * LANES), (3, rows, LANES)) for step in range(count)
    ]
    incoming = [send(part, -1, step, shape) for step, part in enumerate(outgoing)]

    inverse_ops, incoming[:2] = lax.optimization_barrier((inverse_ops, incoming[:2]))
    ops, gains, base, *mirrored = pl.pallas_call(
        functools.partial(prepare_kernel, count, rows),
        out_shape=[jax.ShapeDtypeStruct((2, ny, 3 * ny), jnp.bfloat16), wide, wide] + [part] * count,
        in_specs=[smem] + [vmem] * 4,
        out_specs=[vmem] * (3 + count),
        compiler_params=limit,
        cost_estimate=pl.CostEstimate(flops=10**8, bytes_accessed=4 << 20, transcendentals=0),
        name="prepare",
    )(wall, mirror_blocks, end, gain, inverse_ops)

    mirrored[1], incoming[2] = lax.optimization_barrier((mirrored[1], incoming[2]))
    mirrored = mirrored[:1] + [send(part, 1, i, shape) for i, part in enumerate(mirrored) if i]
    mirrored[0], mirrored[-1] = lax.optimization_barrier((mirrored[0], mirrored[-1]))
    mirrored[0] = send(mirrored[0], 1, 0, shape)

    adjoint = pl.pallas_call(
        functools.partial(adjoint_kernel, count, rows),
        out_shape=[part] * count,
        in_specs=[smem, smem] + [vmem] * (4 + count),
        out_specs=[vmem] * count,
        scratch_shapes=[pltpu.VMEM((3 * ny, 2 * LANES), jnp.bfloat16)] * 2
        + [pltpu.VMEM((ny, 2 * LANES), jnp.float32)] * 2,
        compiler_params=limit,
        cost_estimate=pl.CostEstimate(flops=4 * 10**9, bytes_accessed=4 << 20, transcendentals=0),
        name="adjoint",
    )(wall, slab_steps, mirror_blocks, ops, gains, base, *incoming)
    returned = [adjoint[0]] + [send(adjoint[step], 0, step, shape) for step in range(1, count)]

    offset = pl.pallas_call(
        functools.partial(offset_kernel, count),
        out_shape=jax.ShapeDtypeStruct(start.shape, jnp.float32),
        in_specs=[smem, vmem] + [vmem] * count,
        out_specs=vmem,
        compiler_params=limit,
        cost_estimate=pl.CostEstimate(flops=10**6, bytes_accessed=40 << 20, transcendentals=0),
        name="offset",
    )(wall, start, *mirrored[::-1])
    gradient = pl.pallas_call(
        functools.partial(combine_kernel, count),
        out_shape=jax.ShapeDtypeStruct(start.shape, jnp.float32),
        in_specs=[smem, vmem] + [vmem] * count,
        out_specs=pl.BlockSpec(memory_space=pl.ANY),
        scratch_shapes=[pltpu.VMEM(start.shape, jnp.float32), pltpu.SemaphoreType.DMA((3,))],
        compiler_params=limit,
        cost_estimate=pl.CostEstimate(flops=10**6, bytes_accessed=3 << 20, transcendentals=0),
        name="combine",
    )(wall, offset, *[returned[step] for step in return_order(count)])
    return gradient[None]


def solution(mesh):
    in_specs = (
        P("tm", None, "wall", None),
        P("tm", None, None, "wall"),
        P("tm", None, None, "wall"),
        P("wall", None, None),
        P(),
        P("tm"),
    )
    out_specs = P("tm", None, "wall", None)
    shape = (mesh.shape["tm"], mesh.shape["wall"])
    return jax.shard_map(
        functools.partial(on_device, shape),
        mesh=mesh,
        in_specs=in_specs,
        out_specs=out_specs,
        check_vma=False,
    )
```
